512 devices in a mesh: section: 16 (over z_hi, x), dp: 32 (over y, z_lo, core).
Axes of the slice: x: 4, y: 8, z: 8 (z_hi: 4, z_lo: 2; z = z_hi * 2 + z_lo), core: 2. Of those that a mesh axis runs over, the one named last changes fastest.
Arguments:
- memory: bfloat16 [64, 8, 2048], P('dp', None, 'section'), may hold values from -8 to 8, as said below
- decoder_in: bfloat16 [64, 64, 2048], P('dp'), may hold values from -6 to 6
- key_weight: bfloat16 [16, 2048, 2048], P('section', None, 'dp'), may hold values from -0.125 to 0.125
- value_weight: bfloat16 [16, 2048, 2048], P('section', None, 'dp'), may hold values from -0.125 to 0.125
- top_grad: bfloat16 [64, 64, 2048], P('dp'), may hold values from -6 to 6
Outputs:
- memory_grad: float32 [512, 2048], P(('section', 'dp'))
The draws below stay inside these ranges and needn't reach their ends.
Inputs may be any that keep to these rules, and one draw needn't show every extreme that they name: real-valued memory.
All inputs are finite; a program needn't handle non-finite values.
Results may differ from the reference program's by a relative error of at most 0.03.
Values may be sent and summed in bfloat16 or wider, within the bound.
No kernel may reach another device: no remote copies, remote signals or barrier semaphores. Data moves between devices by JAX's collectives and lax.ppermute only.
A program may use at most 64 MiB of HBM per device.

```python
import jax
import jax.numpy as jnp
from jax import lax

D = 2048
HEADS = 16
HEAD_DIMENSION = 128
TGT = 64
MEM = 8
INNER = 2048
BATCH = 64
N_SECTION = 16


def draw_memory(key, part):
    key = jax.random.fold_in(key, 7)
    first = jax.random.fold_in(key, 0)
    base = jax.random.normal(first, (BATCH, MEM, D), jnp.float32)
    return jnp.clip(base, -6.0, 6.0).astype(jnp.bfloat16)


def steps_of(stream_key, extent, shards, smallest, largest):
    factor_of = 1.0
    for position, blocks in shards:
        draws = jax.random.uniform(jax.random.fold_in(jax.random.fold_in(stream_key, 6), position), (blocks,), jnp.float32, smallest / len(shards), largest / len(shards))
        factor_of = factor_of * jnp.repeat(jnp.exp(draws), extent[position] // blocks).reshape((-1,) + (1,) * (len(extent) - 1 - position))
    return factor_of


def gaussian(own_key, dims, deviation, reach, cuts=(), dtype=jnp.bfloat16):
    entries = jax.random.normal(own_key, dims, jnp.float32) * deviation
    if len(cuts) > 0:
        entries = steps_of(own_key, dims, cuts, -0.22, 0.18) * entries
    return jnp.clip(entries, min=-reach, max=reach).astype(dtype)


def setup_inputs(seed: int = 0) -> dict:
    splits = jax.random.split(jax.random.key(seed), 6)
    memory = draw_memory(jax.random.fold_in(splits[5], 71), 0)
    decoder_in = gaussian(splits[1], (BATCH, TGT, INNER), 1.0, 6.0, ((0, 32),))
    key_weight = gaussian(splits[2], (N_SECTION, D, INNER), D ** -0.5, 0.125, ((0, 16), (2, 32)))
    value_weight = gaussian(splits[3], (N_SECTION, D, INNER), D ** -0.5, 0.125, ((0, 16), (2, 32)))
    top_grad = gaussian(splits[4], (BATCH, TGT, INNER), 1.0, 6.0, ((0, 32),))
    return {"memory": memory, "decoder_in": decoder_in, "key_weight": key_weight, "value_weight": value_weight, "top_grad": top_grad}


def attend(hidden, keys, values):
    tokens = hidden.shape[0]
    scale = lax.rsqrt(lax.optimization_barrier(jnp.mean(hidden * hidden, axis=-1, keepdims=True)) + 1e-06)
    query_rows = (hidden * scale).reshape(tokens, HEADS, -1)
    key_head_split = keys.reshape(keys.shape[0], HEADS, -1)
    value_head_split = values.reshape(values.shape[0], HEADS, -1)
    score_matrix = jnp.einsum('qig,rig->iqr', query_rows, key_head_split, precision=lax.Precision.HIGHEST) / jnp.sqrt(jnp.float32(HEAD_DIMENSION))
    attention_weights = jax.nn.softmax(score_matrix, axis=-1)
    mixed_values = jnp.einsum('xrl,lxz->rxz', attention_weights, value_head_split, precision=lax.Precision.HIGHEST)
    return hidden + mixed_values.reshape(tokens, -1)

def project(memory, weight):
    flat = memory.reshape(-1, memory.shape[2])
    return jnp.dot(flat, weight, preferred_element_type=jnp.float32).astype(jnp.bfloat16).reshape(memory.shape[0], memory.shape[1], -1)

def reference(memory, decoder_in, key_weight, value_weight, top_grad):
    batched = jax.vmap(attend)
    hidden = decoder_in
    stash = []
    for section in range(N_SECTION):
        keys = project(memory, key_weight[section]).astype(jnp.float32)
        values = project(memory, value_weight[section]).astype(jnp.float32)
        stash.append(hidden)
        hidden = batched(hidden.astype(jnp.float32), keys, values).astype(jnp.bfloat16)
    grad = top_grad
    total = jnp.zeros((memory.shape[0] * memory.shape[1], memory.shape[2]), jnp.float32)
    for section in range(N_SECTION - 1, -1, -1):
        keys = project(memory, key_weight[section]).astype(jnp.float32)
        values = project(memory, value_weight[section]).astype(jnp.float32)
        result, pull = jax.vjp(batched, stash[section].astype(jnp.float32), keys, values)
        grad_hidden, grad_keys, grad_values = pull(grad.astype(jnp.float32))
        grad = grad_hidden.astype(jnp.bfloat16)
        flat_keys = grad_keys.reshape(-1, grad_keys.shape[2]).astype(jnp.bfloat16)
        flat_values = grad_values.reshape(-1, grad_values.shape[2]).astype(jnp.bfloat16)
        total = total + jnp.dot(flat_keys, key_weight[section].T, preferred_element_type=jnp.float32)
        total = total + jnp.dot(flat_values, value_weight[section].T, preferred_element_type=jnp.float32)
    return total
```

```python
import functools

import jax
import jax.numpy as jnp
from jax import lax
from jax.experimental import pallas as pl
from jax.experimental.pallas import tpu as pltpu
from jax.sharding import Mesh
from jax.sharding import PartitionSpec as P

HEADS = 16
HEAD_DIMENSION = 128
SECTIONS = 16
MEM = 8
TOKENS = 8
WIDTH = HEADS * HEAD_DIMENSION
LANES = MEM * HEADS
SECTION = ("zh", "x")
DP = ("y", "zl", "c")
RING = ("zh", "x", "y")
F32 = jnp.float32
BF16 = jnp.bfloat16


def wide_dot(a, b):
    return lax.dot_general(a, b, (((1,), (0,)), ((), ())), preferred_element_type=F32)


def rows_dot(a, b):
    return lax.dot_general(a, b, (((1,), (1,)), ((), ())), preferred_element_type=F32)


def two_parts(x):
    high = x.astype(BF16)
    low = (x - high.astype(F32)).astype(BF16)
    return jnp.concatenate([high, low], axis=0)


def exact_dot(x, b):
    both = wide_dot(two_parts(x), b)
    return both[:TOKENS] + both[TOKENS:]


def over_memory(x, combine):
    for shift in (64, 32, 16):
        x = combine(x, pltpu.roll(x, shift, axis=1))
    return x


def chain_kernel(h_ref, g_ref, kv_ref, out_ref, kd, vd, hs, gs, sc_s, p_s, ds_s, scale_s, turned):
    root = HEAD_DIMENSION**-0.5

    def spread(section):
        head_row = lax.broadcasted_iota(jnp.int32, (HEADS, 256), 0)
        lane_head = lax.broadcasted_iota(jnp.int32, (HEADS, 256), 1) >> 7
        for block in range(8):
            own = head_row == lane_head + 2 * block
            for offset, target in ((0, kd), (256, vd)):
                part = kv_ref[section, block, :, offset : offset + 256].astype(F32)
                for m in range(MEM):
                    row = jnp.broadcast_to(part[m : m + 1], (HEADS, 256))
                    target[section, m * HEADS : (m + 1) * HEADS, block * 256 : (block + 1) * 256] = (
                        jnp.where(own, row, 0.0).astype(BF16)
                    )

    spread(0)
    state = h_ref[...]
    for s in range(SECTIONS):
        wide = state.astype(F32)
        hs[s] = wide
        raw = rows_dot(state, kd[s])
        scale = lax.rsqrt(jnp.mean(wide * wide, axis=-1, keepdims=True) + 1e-06)
        scores = raw * (scale * root)
        e = jnp.exp(scores - over_memory(scores, jnp.maximum))
        p = e / over_memory(e, jnp.add)
        sc_s[s] = scores
        p_s[s] = p
        scale_s[s] = jnp.broadcast_to(scale, (TOKENS, LANES))
        if s + 1 < SECTIONS:
            spread(s + 1)
            state = (wide + exact_dot(p, vd[s])).astype(BF16)

    grad = g_ref[...]
    for s in reversed(range(SECTIONS)):
        wide = grad.astype(F32)
        gs[s] = wide
        p = p_s[s]
        dp = rows_dot(grad, vd[s])
        ds = p * (dp - over_memory(p * dp, jnp.add))
        scale = scale_s[s][:, :1]
        ds_s[s] = ds * (scale_s[s] * root)
        if s > 0:
            along = jnp.sum(ds * sc_s[s], axis=-1, keepdims=True) * (1.0 / WIDTH)
            du = exact_dot(ds * root, kd[s])
            grad = (wide + scale * (du - hs[s] * (scale * along))).astype(BF16)

    row_section = lax.broadcasted_iota(jnp.int32, (LANES, LANES), 0) >> 3
    lane_section = lax.broadcasted_iota(jnp.int32, (LANES, LANES), 1) >> 3
    same = row_section == lane_section
    for coefficients, factors, offset in ((ds_s, hs, 0), (p_s, gs, 256)):
        turned[...] = coefficients[...].reshape(SECTIONS * TOKENS, LANES).T
        for head in range(HEADS):
            mine = turned[pl.ds(head, MEM, stride=HEADS), :]
            spread_out = jnp.broadcast_to(mine[None], (SECTIONS, MEM, LANES)).reshape(LANES, LANES)
            left = jnp.where(same, spread_out, 0.0).astype(BF16)
            lanes = slice(head * 128, head * 128 + 128)
            right = factors[:, :, lanes].reshape(SECTIONS * TOKENS, 128).astype(BF16)
            result = wide_dot(left, right).astype(BF16).reshape(SECTIONS, MEM, 128)
            start = offset + (head % 2) * 128
            out_ref[:, head // 2, :, start : start + 128] = result


def chain(h, g, kv):
    vmem = pl.BlockSpec(memory_space=pltpu.VMEM)
    return pl.pallas_call(
        chain_kernel,
        out_shape=jax.ShapeDtypeStruct((SECTIONS, 8, MEM, 512), BF16),
        in_specs=[vmem] * 3,
        out_specs=vmem,
        scratch_shapes=[
            pltpu.VMEM((SECTIONS, LANES, WIDTH), BF16),
            pltpu.VMEM((SECTIONS, LANES, WIDTH), BF16),
            pltpu.VMEM((SECTIONS, TOKENS, WIDTH), F32),
            pltpu.VMEM((SECTIONS, TOKENS, WIDTH), F32),
            pltpu.VMEM((SECTIONS, TOKENS, LANES), F32),
            pltpu.VMEM((SECTIONS, TOKENS, LANES), F32),
            pltpu.VMEM((SECTIONS, TOKENS, LANES), F32),
            pltpu.VMEM((SECTIONS, TOKENS, LANES), F32),
            pltpu.VMEM((LANES, LANES), F32),
        ],
        compiler_params=pltpu.CompilerParams(vmem_limit_bytes=48 * 1024 * 1024),
        name="sections",
    )(h, g, kv)


def swap(block, axis):
    return lax.ppermute(block, axis, [(0, 1), (1, 0)])


def exchange(block, axes):
    return lax.all_to_all(block, axes, split_axis=0, concat_axis=0, tiled=True)


def in_order(blocks, zl, c):
    a, b, d, e = blocks
    a, b = jnp.where(c == 0, a, b), jnp.where(c == 0, b, a)
    d, e = jnp.where(c == 0, d, e), jnp.where(c == 0, e, d)
    low = zl == 0
    return [jnp.where(low, a, d), jnp.where(low, b, e), jnp.where(low, d, a), jnp.where(low, e, b)]


def owner_route():
    route = []
    for slot in range(128):
        for member in range(4):
            y, k = divmod(slot, 16)
            route.append((slot * 4 + member, (y * 4 + member) * 16 + k))
    return route


def body(memory, decoder_in, key_weight, value_weight, top_grad):
    place = lax.axis_index(SECTION)
    zl, c = lax.axis_index("zl"), lax.axis_index("c")

    own = jnp.concatenate([key_weight[0], value_weight[0]], axis=1)
    far = swap(own, "zl")
    weights = [own, swap(own, "c"), far, swap(far, "c")]

    piece = memory.reshape(1, 16, 128)
    every = exchange(jnp.broadcast_to(piece, (128, 16, 128)), RING)
    rows = every.reshape(16, 8, 16, 128).transpose(1, 2, 0, 3).reshape(128, 2048)
    parts = [jnp.dot(rows, w, preferred_element_type=F32).astype(BF16) for w in weights]
    parts = in_order(parts, zl, c)
    projected = jnp.concatenate([q[:, :64] for q in parts] + [q[:, 64:] for q in parts], axis=1)

    columns = exchange(projected.reshape(8, 16, 512), "y")
    columns = columns.reshape(8, 2, MEM, 512).transpose(1, 0, 2, 3)
    outgoing = jnp.broadcast_to(columns[:, None], (2, 8, 8, MEM, 512)).reshape(16, 8, MEM, 512)
    kv = exchange(outgoing, SECTION)

    start = (place % 8) * TOKENS
    mine = (place // 8, start, 0)
    h = lax.dynamic_slice(decoder_in, mine, (1, TOKENS, WIDTH))[0]
    g = lax.dynamic_slice(top_grad, mine, (1, TOKENS, WIDTH))[0]
    grads = chain(h, g, kv)

    shares = exchange(grads, SECTION).reshape(2, 8, 8, MEM, 512)
    summed = jnp.sum(shares.astype(F32), axis=1).astype(BF16)
    back = exchange(summed.transpose(1, 0, 2, 3), "y").reshape(128, 512)
    quarters = [
        jnp.concatenate([back[:, 64 * i : 64 * i + 64], back[:, 256 + 64 * i : 320 + 64 * i]], axis=1)
        for i in range(4)
    ]
    quarters = in_order(quarters, zl, c)
    term = sum(rows_dot(q, w) for q, w in zip(quarters, weights))
    pieces = exchange(term.astype(BF16).reshape(128, 1, 2048), RING)
    total = jnp.sum(pieces.astype(F32), axis=0)
    return lax.ppermute(total, RING + ("zl", "c"), owner_route())


def solution(mesh):
    fine = Mesh(mesh.devices.reshape(4, 4, 8, 2, 2), ("zh", "x", "y", "zl", "c"))
    placed = (
        P(DP, None, SECTION),
        P(DP, None, None),
        P(SECTION, None, DP),
        P(SECTION, None, DP),
        P(DP, None, None),
    )
    return jax.shard_map(
        body, mesh=fine, in_specs=placed, out_specs=P(SECTION + DP, None), check_vma=False
    )
```

```python
import jax
import jax.numpy as jnp
from jax import lax
from jax.experimental import pallas as pl
from jax.experimental.pallas import tpu as pltpu
from jax.sharding import Mesh
from jax.sharding import PartitionSpec as P

HEADS = 16
HEAD_DIMENSION = 128
SECTIONS = 16
MEM = 8
TOKENS = 8
WIDTH = HEADS * HEAD_DIMENSION
LANES = MEM * HEADS
SECTION = ("zh", "x")
DP = ("y", "zl", "c")
RING = ("zh", "x", "y")
MEM_ORDER = [4 * m2 + 2 * zl + c for zl in range(2) for c in range(2) for m2 in range(2)]
F32 = jnp.float32
BF16 = jnp.bfloat16


def wide_dot(a, b):
    return lax.dot_general(a, b, (((1,), (0,)), ((), ())), preferred_element_type=F32)


def rows_dot(a, b):
    return lax.dot_general(a, b, (((1,), (1,)), ((), ())), preferred_element_type=F32)


def two_parts(x):
    high = x.astype(BF16)
    low = (x - high.astype(F32)).astype(BF16)
    return jnp.concatenate([high, low], axis=0)


def exact_dot(x, b):
    both = wide_dot(two_parts(x), b)
    return both[:TOKENS] + both[TOKENS:]


def over_memory(x, combine):
    for shift in (64, 32, 16):
        x = combine(x, pltpu.roll(x, shift, axis=1))
    return x


def slot(section):
    return section % 4 * 4 + section // 4


def chain_kernel(h_ref, g_ref, kv_ref, out_ref, kd, vd, hs, gs, sc_s, p_s, ds_s, scale_s, turned):
    root = HEAD_DIMENSION**-0.5

    def spread(section):
        head_row = lax.broadcasted_iota(jnp.int32, (HEADS, 256), 0)
        lane_head = lax.broadcasted_iota(jnp.int32, (HEADS, 256), 1) >> 7
        for block in range(8):
            own = head_row == lane_head + 2 * block
            for offset, target in ((0, kd), (256, vd)):
                part = kv_ref[slot(section), block, :, offset : offset + 256].astype(F32)
                for i, m in enumerate(MEM_ORDER):
                    row = jnp.broadcast_to(part[m : m + 1], (HEADS, 256))
                    target[section, i * HEADS : (i + 1) * HEADS, block * 256 : (block + 1) * 256] = (
                        jnp.where(own, row, 0.0).astype(BF16)
                    )

    spread(0)
    state = h_ref[...]
    for s in range(SECTIONS):
        wide = state.astype(F32)
        hs[s] = wide
        raw = rows_dot(state, kd[s])
        scale = lax.rsqrt(jnp.mean(wide * wide, axis=-1, keepdims=True) + 1e-06)
        scores = raw * (scale * root)
        e = jnp.exp(scores - over_memory(scores, jnp.maximum))
        p = e / over_memory(e, jnp.add)
        sc_s[s] = scores
        p_s[s] = p
        scale_s[s] = jnp.broadcast_to(scale, (TOKENS, LANES))
        if s + 1 < SECTIONS:
            spread(s + 1)
            state = (wide + exact_dot(p, vd[s])).astype(BF16)

    grad = g_ref[...]
    for s in reversed(range(SECTIONS)):
        wide = grad.astype(F32)
        gs[s] = wide
        p = p_s[s]
        dp = rows_dot(grad, vd[s])
        ds = p * (dp - over_memory(p * dp, jnp.add))
        scale = scale_s[s][:, :1]
        ds_s[s] = ds * (scale_s[s] * root)
        if s > 0:
            along = jnp.sum(ds * sc_s[s], axis=-1, keepdims=True) * (1.0 / WIDTH)
            du = exact_dot(ds * root, kd[s])
            grad = (wide + scale * (du - hs[s] * (scale * along))).astype(BF16)

    row_section = lax.broadcasted_iota(jnp.int32, (LANES, LANES), 0) >> 3
    lane_section = lax.broadcasted_iota(jnp.int32, (LANES, LANES), 1) >> 3
    same = row_section == lane_section
    for coefficients, factors, offset in ((ds_s, hs, 0), (p_s, gs, 256)):
        turned[...] = coefficients[...].reshape(SECTIONS * TOKENS, LANES).T
        for head in range(HEADS):
            mine = turned[pl.ds(head, MEM, stride=HEADS), :]
            spread_out = jnp.broadcast_to(mine[None], (SECTIONS, MEM, LANES)).reshape(LANES, LANES)
            left = jnp.where(same, spread_out, 0.0).astype(BF16)
            lanes = slice(head * 128, head * 128 + 128)
            right = factors[:, :, lanes].reshape(SECTIONS * TOKENS, 128).astype(BF16)
            result = wide_dot(left, right).astype(BF16).reshape(SECTIONS, MEM, 128)
            start = offset + (head % 2) * 128
            for s in range(SECTIONS):
                out_ref[slot(s), head // 2, :, start : start + 128] = result[s]


def chain(h, g, kv):
    vmem = pl.BlockSpec(memory_space=pltpu.VMEM)
    return pl.pallas_call(
        chain_kernel,
        out_shape=jax.ShapeDtypeStruct((SECTIONS, 8, MEM, 512), BF16),
        in_specs=[vmem] * 3,
        out_specs=vmem,
        scratch_shapes=[
            pltpu.VMEM((SECTIONS, LANES, WIDTH), BF16),
            pltpu.VMEM((SECTIONS, LANES, WIDTH), BF16),
            pltpu.VMEM((SECTIONS, TOKENS, WIDTH), F32),
            pltpu.VMEM((SECTIONS, TOKENS, WIDTH), F32),
            pltpu.VMEM((SECTIONS, TOKENS, LANES), F32),
            pltpu.VMEM((SECTIONS, TOKENS, LANES), F32),
            pltpu.VMEM((SECTIONS, TOKENS, LANES), F32),
            pltpu.VMEM((SECTIONS, TOKENS, LANES), F32),
            pltpu.VMEM((LANES, LANES), F32),
        ],
        compiler_params=pltpu.CompilerParams(vmem_limit_bytes=48 * 1024 * 1024),
        name="sections",
    )(h, g, kv)


def swap(block, axis):
    return lax.ppermute(block, axis, [(0, 1), (1, 0)])


def exchange(block, axes):
    return lax.all_to_all(block, axes, split_axis=0, concat_axis=0, tiled=True)


def in_order(blocks, zl, c):
    a, b, d, e = blocks
    a, b = jnp.where(c == 0, a, b), jnp.where(c == 0, b, a)
    d, e = jnp.where(c == 0, d, e), jnp.where(c == 0, e, d)
    low = zl == 0
    return [jnp.where(low, a, d), jnp.where(low, b, e), jnp.where(low, d, a), jnp.where(low, e, b)]


def body(memory, decoder_in, key_weight, value_weight, top_grad):
    zh, x = lax.axis_index("zh"), lax.axis_index("x")
    zl, c = lax.axis_index("zl"), lax.axis_index("c")

    own = jnp.concatenate([key_weight[0], value_weight[0]], axis=1)
    near = swap(own, "c")
    far = swap(own, "zl")
    weights = [own, near, far, swap(far, "c")]

    piece, near = lax.optimization_barrier((memory.reshape(1, 16, 128), near))
    every = exchange(jnp.broadcast_to(piece, (128, 16, 128)), RING)
    rows = every.reshape(16, 8, 16, 128).transpose(1, 2, 0, 3).reshape(128, 2048)
    parts = [jnp.dot(rows, w, preferred_element_type=F32).astype(BF16) for w in weights]
    parts = in_order(parts, zl, c)
    projected = jnp.concatenate([q[:, :64] for q in parts] + [q[:, 64:] for q in parts], axis=1)

    columns = projected.reshape(8, 2, MEM, 512).transpose(1, 0, 2, 3)
    outgoing = jnp.broadcast_to(columns[:, None], (2, 2, 8, MEM, 512)).reshape(32, MEM, 512)
    held = exchange(outgoing, ("zh", "y")).reshape(1, 4, 8, MEM, 512)
    kv = exchange(jnp.broadcast_to(held, (4, 4, 8, MEM, 512)), "x").reshape(16, 8, MEM, 512)

    mine = (zh // 2, (zh % 2 * 4 + x) * TOKENS, 0)
    h = lax.dynamic_slice(decoder_in, mine, (1, TOKENS, WIDTH))[0]
    g = lax.dynamic_slice(top_grad, mine, (1, TOKENS, WIDTH))[0]
    grads = chain(h, g, kv)

    shares = exchange(grads.reshape(4, 4, 8, MEM, 512), "x")
    summed = jnp.sum(shares.astype(F32), axis=0).astype(BF16)
    halves = exchange(summed.reshape(64, 4, 512), ("zh", "y", "zl"))
    halves = halves.reshape(2, 2, 8, 2, 2, 2, 512).astype(F32)
    summed = jnp.sum(halves, axis=1).astype(BF16)
    kept = jnp.where(c == 0, summed[:, :, :, 0], summed[:, :, :, 1])
    given = jnp.where(c == 0, summed[:, :, :, 1], summed[:, :, :, 0])
    got = swap(given, "c")
    first, second = jnp.where(c == 0, kept, got), jnp.where(c == 0, got, kept)
    back = jnp.stack([first, second]).transpose(2, 3, 0, 1, 4, 5).reshape(128, 512)
    quarters = [
        jnp.concatenate([back[:, 64 * i : 64 * i + 64], back[:, 256 + 64 * i : 320 + 64 * i]], axis=1)
        for i in range(4)
    ]
    quarters = in_order(quarters, zl, c)
    term = sum(rows_dot(q, w) for q, w in zip(quarters, weights))
    pieces = exchange(term.astype(BF16).reshape(128, 1, 2048), RING)
    return jnp.sum(pieces.astype(F32), axis=0)


def solution(mesh):
    fine = Mesh(mesh.devices.reshape(4, 4, 8, 2, 2), ("zh", "x", "y", "zl", "c"))
    placed = (
        P(DP, None, SECTION),
        P(DP, None, None),
        P(SECTION, None, DP),
        P(SECTION, None, DP),
        P(DP, None, None),
    )
    return jax.shard_map(
        body, mesh=fine, in_specs=placed, out_specs=P(SECTION + DP, None), check_vma=False
    )
```

```python
import jax
import jax.numpy as jnp
from jax import lax
from jax.experimental import pallas as pl
from jax.experimental.pallas import tpu as pltpu
from jax.sharding import Mesh
from jax.sharding import PartitionSpec as P

HEADS = 16
HEAD_DIMENSION = 128
SECTIONS = 16
MEM = 8
TOKENS = 8
WIDTH = HEADS * HEAD_DIMENSION
LANES = MEM * HEADS
SECTION = ("zh", "x")
DP = ("yh", "yl", "zl", "c")
BLOCK = ("yh", "zl")
RING = SECTION + BLOCK
F32 = jnp.float32
BF16 = jnp.bfloat16


def wide_dot(a, b):
    return lax.dot_general(a, b, (((1,), (0,)), ((), ())), preferred_element_type=F32)


def rows_dot(a, b):
    return lax.dot_general(a, b, (((1,), (1,)), ((), ())), preferred_element_type=F32)


def two_parts(x):
    high = x.astype(BF16)
    low = (x - high.astype(F32)).astype(BF16)
    return jnp.concatenate([high, low], axis=0)


def exact_dot(x, b):
    both = wide_dot(two_parts(x), b)
    return both[:TOKENS] + both[TOKENS:]


def others(x):
    return [pltpu.roll(x, k * HEADS, axis=1) for k in range(1, MEM)]


def tree(terms):
    while len(terms) > 1:
        terms = [a + b for a, b in zip(terms[::2], terms[1::2])] + terms[len(terms) // 2 * 2 :]
    return terms[0]


def slot(section):
    return section % 4 * 4 + section // 4


def head_place(head):
    yh, yl, zl = head // 4, head // 2 % 2, head % 2
    return yh * 2 + zl, yl * 128


def chain_kernel(h_ref, g_ref, kv_ref, out_ref, left, right, key_rows, value_rows, hs, gs, sc_s, p_s, ds_s, scale_s, turned):
    root = HEAD_DIMENSION**-0.5
    lane_head = lax.broadcasted_iota(jnp.int32, (LANES, LANES), 1) % HEADS
    row_head = lax.broadcasted_iota(jnp.int32, (LANES, LANES), 0) % HEADS

    def fill(section, turned_offset, straight_offset):
        now = section % 2
        for head in range(HEADS):
            block, lane = head_place(head)
            own = pl.ds(head, MEM, stride=HEADS)
            for offset, target in ((turned_offset, key_rows), (straight_offset, value_rows)):
                start = offset + lane
                target[now, own, :] = kv_ref[slot(section), block, :, start : start + 128].astype(F32)
        columns = key_rows[now].T
        rows = value_rows[now]
        for head in range(HEADS):
            lanes = slice(head * 128, head * 128 + 128)
            left[now, lanes, :] = jnp.where(lane_head == head, columns, 0.0).astype(BF16)
            right[now, :, lanes] = jnp.where(row_head == head, rows, 0.0).astype(BF16)

    fill(0, 0, 256)
    state = h_ref[...]
    for s in range(SECTIONS):
        wide = state.astype(F32)
        hs[s] = wide
        raw = wide_dot(state, left[s % 2])
        scale = lax.rsqrt(jnp.mean(wide * wide, axis=-1, keepdims=True) + 1e-06)
        scores = raw * (scale * root)
        ratios = [jnp.exp(jnp.minimum(o - scores, 80.0)) for o in others(scores)]
        p = 1.0 / (1.0 + tree(ratios))
        sc_s[s] = scores
        p_s[s] = p
        scale_s[s] = jnp.broadcast_to(scale, (TOKENS, LANES))
        if s + 1 < SECTIONS:
            fill(s + 1, 0, 256)
            state = (wide + exact_dot(p, right[s % 2])).astype(BF16)

    fill(SECTIONS - 1, 256, 0)
    grad = g_ref[...]
    for s in reversed(range(SECTIONS)):
        wide = grad.astype(F32)
        gs[s] = wide
        p = p_s[s]
        dp = wide_dot(grad, left[s % 2])
        weighted = p * dp
        ds = p * (dp - tree([weighted] + others(weighted)))
        scale = scale_s[s][:, :1]
        ds_s[s] = ds * (scale_s[s] * root)
        if s > 0:
            fill(s - 1, 256, 0)
            along = jnp.sum(ds * sc_s[s], axis=-1, keepdims=True) * (1.0 / WIDTH)
            du = exact_dot(ds * root, right[s % 2])
            grad = (wide + scale * (du - hs[s] * (scale * along))).astype(BF16)

    row_section = lax.broadcasted_iota(jnp.int32, (LANES, LANES), 0) >> 3
    lane_section = lax.broadcasted_iota(jnp.int32, (LANES, LANES), 1) >> 3
    same = row_section == lane_section
    for coefficients, factors, offset in ((ds_s, hs, 0), (p_s, gs, 256)):
        turned[...] = coefficients[...].reshape(SECTIONS * TOKENS, LANES).T
        for head in range(HEADS):
            mine = turned[pl.ds(head, MEM, stride=HEADS), :]
            spread_out = jnp.broadcast_to(mine[None], (SECTIONS, MEM, LANES)).reshape(LANES, LANES)
            left = jnp.where(same, spread_out, 0.0).astype(BF16)
            lanes = slice(head * 128, head * 128 + 128)
            right = factors[:, :, lanes].reshape(SECTIONS * TOKENS, 128).astype(BF16)
            result = wide_dot(left, right).astype(BF16).reshape(SECTIONS, MEM, 128)
            block, lane = head_place(head)
            start = offset + lane
            for s in range(SECTIONS):
                out_ref[slot(s), block, :, start : start + 128] = result[s]


def chain(h, g, kv):
    vmem = pl.BlockSpec(memory_space=pltpu.VMEM)
    return pl.pallas_call(
        chain_kernel,
        out_shape=jax.ShapeDtypeStruct((SECTIONS, 8, MEM, 512), BF16),
        in_specs=[vmem] * 3,
        out_specs=vmem,
        scratch_shapes=[
            pltpu.VMEM((2, WIDTH, LANES), BF16),
            pltpu.VMEM((2, LANES, WIDTH), BF16),
            pltpu.VMEM((2, LANES, LANES), F32),
            pltpu.VMEM((2, LANES, LANES), F32),
            pltpu.VMEM((SECTIONS, TOKENS, WIDTH), F32),
            pltpu.VMEM((SECTIONS, TOKENS, WIDTH), F32),
            pltpu.VMEM((SECTIONS, TOKENS, LANES), F32),
            pltpu.VMEM((SECTIONS, TOKENS, LANES), F32),
            pltpu.VMEM((SECTIONS, TOKENS, LANES), F32),
            pltpu.VMEM((SECTIONS, TOKENS, LANES), F32),
            pltpu.VMEM((LANES, LANES), F32),
        ],
        compiler_params=pltpu.CompilerParams(vmem_limit_bytes=24 * 1024 * 1024),
        name="sections",
    )(h, g, kv)


def term_kernel(grad_ref, *refs):
    *weight_refs, out_ref, wide = refs
    rows = grad_ref.shape[1]
    for start in range(0, WIDTH, 512):
        columns = slice(start, start + 512)
        total = sum(rows_dot(grad_ref[i], ref[columns, :]) for i, ref in enumerate(weight_refs))
        for lane in range(0, 512, 128):
            wide[pl.ds((start + lane) // 128, rows, stride=HEADS), :] = total[:, lane : lane + 128]
    out_ref[...] = wide[...].astype(BF16).reshape(rows, HEADS, 128)


def term(grads, weights):
    vmem = pl.BlockSpec(memory_space=pltpu.VMEM)
    rows = grads.shape[1]
    return pl.pallas_call(
        term_kernel,
        out_shape=jax.ShapeDtypeStruct((rows, HEADS, 128), BF16),
        in_specs=[vmem] * (1 + len(weights)),
        out_specs=vmem,
        scratch_shapes=[pltpu.VMEM((rows * HEADS, 128), F32)],
        compiler_params=pltpu.CompilerParams(vmem_limit_bytes=24 * 1024 * 1024),
        name="term",
    )(grads, *weights)


def swap(block, axis):
    return lax.ppermute(block, axis, [(0, 1), (1, 0)])


def exchange(block, axes):
    return lax.all_to_all(block, axes, split_axis=0, concat_axis=0, tiled=True)


def in_order(blocks, yl, c):
    a, b, d, e = blocks
    a, b = jnp.where(c == 0, a, b), jnp.where(c == 0, b, a)
    d, e = jnp.where(c == 0, d, e), jnp.where(c == 0, e, d)
    low = yl == 0
    return [jnp.where(low, a, d), jnp.where(low, b, e), jnp.where(low, d, a), jnp.where(low, e, b)]


def body(memory, decoder_in, key_weight, value_weight, top_grad):
    zh, x = lax.axis_index("zh"), lax.axis_index("x")
    yl, c = lax.axis_index("yl"), lax.axis_index("c")

    own = jnp.concatenate([key_weight[0], value_weight[0]], axis=1)
    near = swap(own, "c")
    far = swap(own, "yl")

    piece = memory.reshape(2, 2, 2, 2, 128).transpose(0, 1, 3, 2, 4).reshape(1, 16, 128)
    piece = jnp.broadcast_to(piece, (16, 16, 128))
    wide = exchange(piece, SECTION).transpose(1, 0, 2).reshape(1, 16, 2048)
    wide, near, far = lax.optimization_barrier((wide, near, far))
    weights = [own, near, far, swap(far, "c")]
    rows = exchange(jnp.broadcast_to(wide, (8, 16, 2048)), BLOCK).reshape(128, 2048)
    parts = [jnp.dot(rows, w, preferred_element_type=F32).astype(BF16) for w in weights]
    parts = in_order(parts, yl, c)
    projected = jnp.concatenate([q[:, :64] for q in parts] + [q[:, 64:] for q in parts], axis=1)

    columns = projected.reshape(8, 2, MEM, 512).transpose(1, 0, 2, 3)
    outgoing = jnp.broadcast_to(columns[:, None], (2, 2, 8, MEM, 512)).reshape(32, MEM, 512)
    held = exchange(outgoing, ("zh",) + BLOCK).reshape(1, 4, 8, MEM, 512)
    kv = exchange(jnp.broadcast_to(held, (4, 4, 8, MEM, 512)), "x").reshape(16, 8, MEM, 512)

    mine = (zh // 2, (zh % 2 * 4 + x) * TOKENS, 0)
    h = lax.dynamic_slice(decoder_in, mine, (1, TOKENS, WIDTH))[0]
    g = lax.dynamic_slice(top_grad, mine, (1, TOKENS, WIDTH))[0]
    grads = chain(h, g, kv)

    shares = exchange(grads.reshape(4, 4, 8, MEM, 512), "x")
    summed = jnp.sum(shares.astype(F32), axis=0).astype(BF16)
    parts = exchange(summed.reshape(128, 2, 512), ("zh", "yh", "zl", "yl", "c"))
    parts = jnp.sum(parts.reshape(2, 2, 4, 2, 2, 2, 2, 512).astype(F32), axis=1).astype(BF16)
    back = parts.transpose(1, 3, 2, 4, 0, 5, 6).reshape(128, 2, 4, 64)
    members = [back[:, :, i].reshape(128, 128) for i in range(4)]
    members = jnp.stack(in_order(members, yl, c))
    pieces = exchange(term(members, weights), RING)
    return jnp.sum(pieces.astype(F32), axis=0).reshape(1, WIDTH)


def solution(mesh):
    fine = Mesh(mesh.devices.reshape(4, 4, 4, 2, 2, 2), SECTION + DP)
    placed = (
        P(DP, None, SECTION),
        P(DP, None, None),
        P(SECTION, None, DP),
        P(SECTION, None, DP),
        P(DP, None, None),
    )
    return jax.shard_map(
        body, mesh=fine, in_specs=placed, out_specs=P(SECTION + DP, None), check_vma=False
    )
```

```python
import jax
import jax.numpy as jnp
from jax import lax
from jax.experimental import pallas as pl
from jax.experimental.pallas import tpu as pltpu
from jax.sharding import Mesh
from jax.sharding import PartitionSpec as P

HEADS = 16
HEAD_DIMENSION = 128
SECTIONS = 16
MEM = 8
TOKENS = 8
WIDTH = HEADS * HEAD_DIMENSION
LANES = MEM * HEADS
SECTION = ("zh", "x")
DP = ("yh", "yl", "zl", "c")
BLOCK = ("yh", "zl")
F32 = jnp.float32
BF16 = jnp.bfloat16


def wide_dot(a, b):
    return lax.dot_general(a, b, (((1,), (0,)), ((), ())), preferred_element_type=F32)


def rows_dot(a, b):
    return lax.dot_general(a, b, (((1,), (1,)), ((), ())), preferred_element_type=F32)


def two_parts(x):
    high = x.astype(BF16)
    low = (x - high.astype(F32)).astype(BF16)
    return jnp.concatenate([high, low], axis=0)


def exact_dot(x, b):
    both = wide_dot(two_parts(x), b)
    return both[:TOKENS] + both[TOKENS:]


def others(x):
    return [pltpu.roll(x, k * HEADS, axis=1) for k in range(1, MEM)]


def tree(terms):
    while len(terms) > 1:
        terms = [a + b for a, b in zip(terms[::2], terms[1::2])] + terms[len(terms) // 2 * 2 :]
    return terms[0]


def slot(section):
    return section % 4 * 4 + section // 4


def head_place(head):
    yh, yl, zl = head // 4, head // 2 % 2, head % 2
    return yh * 2 + zl, yl * 128


def chain_kernel(h_ref, g_ref, kv_ref, out_ref, left, right, key_rows, value_rows, hs, gs, sc_s, p_s, ds_s, scale_s, turned):
    root = HEAD_DIMENSION**-0.5
    lane_head = lax.broadcasted_iota(jnp.int32, (LANES, LANES), 1) % HEADS
    row_head = lax.broadcasted_iota(jnp.int32, (LANES, LANES), 0) % HEADS

    def fill(section, turned_offset, straight_offset):
        now = section % 2
        for head in range(HEADS):
            block, lane = head_place(head)
            own = pl.ds(head, MEM, stride=HEADS)
            for offset, target in ((turned_offset, key_rows), (straight_offset, value_rows)):
                start = offset + lane
                target[now, own, :] = kv_ref[slot(section), block, :, start : start + 128].astype(F32)
        columns = key_rows[now].T
        rows = value_rows[now]
        for head in range(HEADS):
            lanes = slice(head * 128, head * 128 + 128)
            left[now, lanes, :] = jnp.where(lane_head == head, columns, 0.0).astype(BF16)
            right[now, :, lanes] = jnp.where(row_head == head, rows, 0.0).astype(BF16)

    fill(0, 0, 256)
    state = h_ref[...]
    for s in range(SECTIONS):
        wide = state.astype(F32)
        hs[s] = wide
        raw = wide_dot(state, left[s % 2])
        scale = lax.rsqrt(jnp.mean(wide * wide, axis=-1, keepdims=True) + 1e-06)
        scores = raw * (scale * root)
        ratios = [jnp.exp(jnp.minimum(o - scores, 80.0)) for o in others(scores)]
        p = 1.0 / (1.0 + tree(ratios))
        sc_s[s] = scores
        p_s[s] = p
        scale_s[s] = jnp.broadcast_to(scale, (TOKENS, LANES))
        if s + 1 < SECTIONS:
            fill(s + 1, 0, 256)
            state = (wide + exact_dot(p, right[s % 2])).astype(BF16)

    fill(SECTIONS - 1, 256, 0)
    grad = g_ref[...]
    for s in reversed(range(SECTIONS)):
        wide = grad.astype(F32)
        gs[s] = wide
        p = p_s[s]
        dp = wide_dot(grad, left[s % 2])
        weighted = p * dp
        ds = p * (dp - tree([weighted] + others(weighted)))
        scale = scale_s[s][:, :1]
        ds_s[s] = ds * (scale_s[s] * root)
        if s > 0:
            fill(s - 1, 256, 0)
            along = jnp.sum(ds * sc_s[s], axis=-1, keepdims=True) * (1.0 / WIDTH)
            du = exact_dot(ds * root, right[s % 2])
            grad = (wide + scale * (du - hs[s] * (scale * along))).astype(BF16)

    row_section = lax.broadcasted_iota(jnp.int32, (LANES, LANES), 0) >> 3
    lane_section = lax.broadcasted_iota(jnp.int32, (LANES, LANES), 1) >> 3
    same = row_section == lane_section
    for coefficients, factors, offset in ((ds_s, hs, 0), (p_s, gs, 256)):
        turned[...] = coefficients[...].reshape(SECTIONS * TOKENS, LANES).T
        for head in range(HEADS):
            mine = turned[pl.ds(head, MEM, stride=HEADS), :]
            spread_out = jnp.broadcast_to(mine[None], (SECTIONS, MEM, LANES)).reshape(LANES, LANES)
            left = jnp.where(same, spread_out, 0.0).astype(BF16)
            lanes = slice(head * 128, head * 128 + 128)
            right = factors[:, :, lanes].reshape(SECTIONS * TOKENS, 128).astype(BF16)
            result = wide_dot(left, right).astype(BF16).reshape(SECTIONS, MEM, 128)
            block, lane = head_place(head)
            start = offset + lane
            for s in range(SECTIONS):
                out_ref[slot(s), block, :, start : start + 128] = result[s]


def chain(h, g, kv):
    vmem = pl.BlockSpec(memory_space=pltpu.VMEM)
    return pl.pallas_call(
        chain_kernel,
        out_shape=jax.ShapeDtypeStruct((SECTIONS, 8, MEM, 512), BF16),
        in_specs=[vmem] * 3,
        out_specs=vmem,
        scratch_shapes=[
            pltpu.VMEM((2, WIDTH, LANES), BF16),
            pltpu.VMEM((2, LANES, WIDTH), BF16),
            pltpu.VMEM((2, LANES, LANES), F32),
            pltpu.VMEM((2, LANES, LANES), F32),
            pltpu.VMEM((SECTIONS, TOKENS, WIDTH), F32),
            pltpu.VMEM((SECTIONS, TOKENS, WIDTH), F32),
            pltpu.VMEM((SECTIONS, TOKENS, LANES), F32),
            pltpu.VMEM((SECTIONS, TOKENS, LANES), F32),
            pltpu.VMEM((SECTIONS, TOKENS, LANES), F32),
            pltpu.VMEM((SECTIONS, TOKENS, LANES), F32),
            pltpu.VMEM((LANES, LANES), F32),
        ],
        compiler_params=pltpu.CompilerParams(vmem_limit_bytes=24 * 1024 * 1024),
        name="sections",
    )(h, g, kv)


def term_kernel(grad_ref, *refs):
    *weight_refs, out_ref, wide = refs
    rows = grad_ref.shape[1]
    for start in range(0, WIDTH, 512):
        columns = slice(start, start + 512)
        total = sum(rows_dot(grad_ref[i], ref[columns, :]) for i, ref in enumerate(weight_refs))
        for lane in range(0, 512, 128):
            wide[pl.ds((start + lane) // 128, rows, stride=HEADS), :] = total[:, lane : lane + 128]
    out_ref[...] = wide[...].astype(BF16).reshape(rows, HEADS, 128)


def term(grads, weights):
    vmem = pl.BlockSpec(memory_space=pltpu.VMEM)
    rows = grads.shape[1]
    return pl.pallas_call(
        term_kernel,
        out_shape=jax.ShapeDtypeStruct((rows, HEADS, 128), BF16),
        in_specs=[vmem] * (1 + len(weights)),
        out_specs=vmem,
        scratch_shapes=[pltpu.VMEM((rows * HEADS, 128), F32)],
        compiler_params=pltpu.CompilerParams(vmem_limit_bytes=24 * 1024 * 1024),
        name="term",
    )(grads, *weights)


def swap(block, axis):
    return lax.ppermute(block, axis, [(0, 1), (1, 0)])


def exchange(block, axes):
    return lax.all_to_all(block, axes, split_axis=0, concat_axis=0, tiled=True)


def in_order(blocks, yl, c):
    a, b, d, e = blocks
    a, b = jnp.where(c == 0, a, b), jnp.where(c == 0, b, a)
    d, e = jnp.where(c == 0, d, e), jnp.where(c == 0, e, d)
    low = yl == 0
    return [jnp.where(low, a, d), jnp.where(low, b, e), jnp.where(low, d, a), jnp.where(low, e, b)]


def body(memory, decoder_in, key_weight, value_weight, top_grad):
    zh, x = lax.axis_index("zh"), lax.axis_index("x")
    yl, c = lax.axis_index("yl"), lax.axis_index("c")

    own = jnp.concatenate([key_weight[0], value_weight[0]], axis=1)
    near = swap(own, "c")
    far = swap(own, "yl")

    piece = memory.reshape(2, 2, 2, 2, 128).transpose(0, 1, 3, 2, 4).reshape(1, 16, 128)
    narrow = exchange(jnp.broadcast_to(piece, (32, 16, 128)), ("zh",) + BLOCK)
    narrow = narrow.reshape(4, 128, 128).transpose(1, 0, 2).reshape(1, 128, 512)
    narrow, near, far = lax.optimization_barrier((narrow, near, far))
    weights = [own, near, far, swap(far, "c")]
    every = exchange(jnp.broadcast_to(narrow, (4, 128, 512)), "x")
    rows = every.reshape(4, 128, 4, 128).transpose(1, 2, 0, 3).reshape(128, 2048)
    parts = [jnp.dot(rows, w, preferred_element_type=F32).astype(BF16) for w in weights]
    parts = in_order(parts, yl, c)
    projected = jnp.concatenate([q[:, :64] for q in parts] + [q[:, 64:] for q in parts], axis=1)

    columns = projected.reshape(8, 2, MEM, 512).transpose(1, 0, 2, 3)
    outgoing = jnp.broadcast_to(columns[:, None], (2, 2, 8, MEM, 512)).reshape(32, MEM, 512)
    held = exchange(outgoing, ("zh",) + BLOCK).reshape(1, 4, 8, MEM, 512)
    kv = exchange(jnp.broadcast_to(held, (4, 4, 8, MEM, 512)), "x").reshape(16, 8, MEM, 512)

    mine = (zh // 2, (zh % 2 * 4 + x) * TOKENS, 0)
    h = lax.dynamic_slice(decoder_in, mine, (1, TOKENS, WIDTH))[0]
    g = lax.dynamic_slice(top_grad, mine, (1, TOKENS, WIDTH))[0]
    grads = chain(h, g, kv)

    shares = exchange(grads.reshape(4, 4, 8, MEM, 512), "x")
    summed = jnp.sum(shares.astype(F32), axis=0).astype(BF16)
    parts = exchange(summed.reshape(128, 2, 512), ("zh", "yh", "zl", "yl", "c"))
    parts = jnp.sum(parts.reshape(2, 2, 4, 2, 2, 2, 2, 512).astype(F32), axis=1).astype(BF16)
    back = parts.transpose(1, 3, 2, 4, 0, 5, 6).reshape(128, 2, 4, 64)
    members = [back[:, :, i].reshape(128, 128) for i in range(4)]
    members = jnp.stack(in_order(members, yl, c))
    pieces = term(members, weights).reshape(4, 4, 8, HEADS, 128).transpose(1, 0, 2, 3, 4)
    pieces = jnp.sum(exchange(pieces, "x").astype(F32), axis=0).astype(BF16)
    pieces = exchange(pieces.reshape(32, HEADS, 128), ("zh",) + BLOCK)
    return jnp.sum(pieces.astype(F32), axis=0).reshape(1, WIDTH)


def solution(mesh):
    fine = Mesh(mesh.devices.reshape(4, 4, 4, 2, 2, 2), SECTION + DP)
    placed = (
        P(DP, None, SECTION),
        P(DP, None, None),
        P(SECTION, None, DP),
        P(SECTION, None, DP),
        P(DP, None, None),
    )
    return jax.shard_map(
        body, mesh=fine, in_specs=placed, out_specs=P(SECTION + DP, None), check_vma=False
    )
```

```python
import jax
import jax.numpy as jnp
from jax import lax
from jax.experimental import pallas as pl
from jax.experimental.pallas import tpu as pltpu
from jax.sharding import Mesh
from jax.sharding import PartitionSpec as P

HEADS = 16
HEAD_DIMENSION = 128
SECTIONS = 16
MEM = 8
TOKENS = 8
WIDTH = HEADS * HEAD_DIMENSION
LANES = MEM * HEADS
SECTION = ("zh", "x")
DP = ("yh", "yl", "zl", "c")
BLOCK = ("yh", "zl")
F32 = jnp.float32
BF16 = jnp.bfloat16


def wide_dot(a, b):
    return lax.dot_general(a, b, (((1,), (0,)), ((), ())), preferred_element_type=F32)


def rows_dot(a, b):
    return lax.dot_general(a, b, (((1,), (1,)), ((), ())), preferred_element_type=F32)


def two_parts(x):
    high = x.astype(BF16)
    low = (x - high.astype(F32)).astype(BF16)
    return jnp.concatenate([high, low], axis=0)


def exact_dot(x, b):
    both = wide_dot(two_parts(x), b)
    return both[:TOKENS] + both[TOKENS:]


def others(x):
    return [pltpu.roll(x, k * HEADS, axis=1) for k in range(1, MEM)]


def tree(terms):
    while len(terms) > 1:
        terms = [a + b for a, b in zip(terms[::2], terms[1::2])] + terms[len(terms) // 2 * 2 :]
    return terms[0]


def slot(section):
    return section % 4 * 4 + section // 4


def head_place(head):
    yh, yl, zl = head // 4, head // 2 % 2, head % 2
    return yh * 2 + zl, yl * 128


def chain_kernel(h_ref, g_ref, kv_ref, out_ref, left, right, key_rows, value_rows, hs, gs, sc_s, p_s, ds_s, scale_s, turned):
    root = HEAD_DIMENSION**-0.5
    lane_head = lax.broadcasted_iota(jnp.int32, (LANES, LANES), 1) % HEADS
    row_head = lax.broadcasted_iota(jnp.int32, (LANES, LANES), 0) % HEADS

    def fill(section, turned_offset, straight_offset):
        now = section % 2
        for head in range(HEADS):
            block, lane = head_place(head)
            own = pl.ds(head, MEM, stride=HEADS)
            for offset, target in ((turned_offset, key_rows), (straight_offset, value_rows)):
                start = offset + lane
                target[now, own, :] = kv_ref[slot(section), block, :, start : start + 128].astype(F32)
        columns = key_rows[now].T
        rows = value_rows[now]
        for head in range(HEADS):
            lanes = slice(head * 128, head * 128 + 128)
            left[now, lanes, :] = jnp.where(lane_head == head, columns, 0.0).astype(BF16)
            right[now, :, lanes] = jnp.where(row_head == head, rows, 0.0).astype(BF16)

    fill(0, 0, 256)
    state = h_ref[...]
    for s in range(SECTIONS):
        wide = state.astype(F32)
        hs[s] = wide
        raw = wide_dot(state, left[s % 2])
        scale = lax.rsqrt(jnp.mean(wide * wide, axis=-1, keepdims=True) + 1e-06)
        scores = raw * (scale * root)
        ratios = [jnp.exp(jnp.minimum(o - scores, 80.0)) for o in others(scores)]
        p = 1.0 / (1.0 + tree(ratios))
        sc_s[s] = scores
        p_s[s] = p
        scale_s[s] = jnp.broadcast_to(scale, (TOKENS, LANES))
        if s + 1 < SECTIONS:
            fill(s + 1, 0, 256)
            state = (wide + exact_dot(p, right[s % 2])).astype(BF16)

    fill(SECTIONS - 1, 256, 0)
    grad = g_ref[...]
    for s in reversed(range(SECTIONS)):
        wide = grad.astype(F32)
        gs[s] = wide
        p = p_s[s]
        dp = wide_dot(grad, left[s % 2])
        weighted = p * dp
        ds = p * (dp - tree([weighted] + others(weighted)))
        scale = scale_s[s][:, :1]
        ds_s[s] = ds * (scale_s[s] * root)
        if s > 0:
            fill(s - 1, 256, 0)
            along = jnp.sum(ds * sc_s[s], axis=-1, keepdims=True) * (1.0 / WIDTH)
            du = exact_dot(ds * root, right[s % 2])
            grad = (wide + scale * (du - hs[s] * (scale * along))).astype(BF16)

    row_section = lax.broadcasted_iota(jnp.int32, (LANES, LANES), 0) >> 3
    lane_section = lax.broadcasted_iota(jnp.int32, (LANES, LANES), 1) >> 3
    same = row_section == lane_section
    for coefficients, factors, offset in ((ds_s, hs, 0), (p_s, gs, 256)):
        turned[...] = coefficients[...].reshape(SECTIONS * TOKENS, LANES).T
        for head in range(HEADS):
            mine = turned[pl.ds(head, MEM, stride=HEADS), :]
            spread_out = jnp.broadcast_to(mine[None], (SECTIONS, MEM, LANES)).reshape(LANES, LANES)
            left = jnp.where(same, spread_out, 0.0).astype(BF16)
            lanes = slice(head * 128, head * 128 + 128)
            right = factors[:, :, lanes].reshape(SECTIONS * TOKENS, 128).astype(BF16)
            result = wide_dot(left, right).astype(BF16).reshape(SECTIONS, MEM, 128)
            block, lane = head_place(head)
            start = offset + lane
            for s in range(SECTIONS):
                out_ref[slot(s), block, :, start : start + 128] = result[s]


def chain(h, g, kv):
    vmem = pl.BlockSpec(memory_space=pltpu.VMEM)
    return pl.pallas_call(
        chain_kernel,
        out_shape=jax.ShapeDtypeStruct((SECTIONS, 8, MEM, 512), BF16),
        in_specs=[vmem] * 3,
        out_specs=vmem,
        scratch_shapes=[
            pltpu.VMEM((2, WIDTH, LANES), BF16),
            pltpu.VMEM((2, LANES, WIDTH), BF16),
            pltpu.VMEM((2, LANES, LANES), F32),
            pltpu.VMEM((2, LANES, LANES), F32),
            pltpu.VMEM((SECTIONS, TOKENS, WIDTH), F32),
            pltpu.VMEM((SECTIONS, TOKENS, WIDTH), F32),
            pltpu.VMEM((SECTIONS, TOKENS, LANES), F32),
            pltpu.VMEM((SECTIONS, TOKENS, LANES), F32),
            pltpu.VMEM((SECTIONS, TOKENS, LANES), F32),
            pltpu.VMEM((SECTIONS, TOKENS, LANES), F32),
            pltpu.VMEM((LANES, LANES), F32),
        ],
        compiler_params=pltpu.CompilerParams(vmem_limit_bytes=24 * 1024 * 1024),
        name="sections",
    )(h, g, kv)


def term_kernel(me_ref, part_ref, *refs):
    *weight_refs, out_ref, wide = refs
    yl_set, c_set = me_ref[0] == 1, me_ref[1] == 1
    halves = part_ref[...].astype(F32).reshape(2, 2, 64, 512)
    summed = (halves[:, 0] + halves[:, 1]).reshape(128, 512)
    blocks = [
        jnp.concatenate([summed[:, 64 * q : 64 * q + 64], summed[:, 256 + 64 * q : 320 + 64 * q]], axis=1)
        for q in range(4)
    ]
    a, b, d, e = blocks
    a, b = jnp.where(c_set, b, a), jnp.where(c_set, a, b)
    d, e = jnp.where(c_set, e, d), jnp.where(c_set, d, e)
    a, b, d, e = jnp.where(yl_set, d, a), jnp.where(yl_set, e, b), jnp.where(yl_set, a, d), jnp.where(yl_set, b, e)
    grads = [q.astype(BF16) for q in (a, b, d, e)]
    for start in range(0, WIDTH, 512):
        columns = slice(start, start + 512)
        total = sum(rows_dot(q, ref[columns, :]) for q, ref in zip(grads, weight_refs))
        for lane in range(0, 512, 128):
            wide[pl.ds((start + lane) // 128, 128, stride=HEADS), :] = total[:, lane : lane + 128]
    for row in range(128):
        j, yh, zl, yl, c, m = (row >> k & n for k, n in ((6, 1), (4, 3), (3, 1), (2, 1), (1, 1), (0, 1)))
        owner = ((yl * 2 + zl) * 4 + yh) * 8 + (c * 2 + j) * 2 + m
        out_ref[owner] = wide[row * HEADS : (row + 1) * HEADS, :].astype(BF16)


def term(me, parts, weights):
    vmem = pl.BlockSpec(memory_space=pltpu.VMEM)
    return pl.pallas_call(
        term_kernel,
        out_shape=jax.ShapeDtypeStruct((128, HEADS, 128), BF16),
        in_specs=[pl.BlockSpec(memory_space=pltpu.SMEM)] + [vmem] * (1 + len(weights)),
        out_specs=vmem,
        scratch_shapes=[pltpu.VMEM((128 * HEADS, 128), F32)],
        compiler_params=pltpu.CompilerParams(vmem_limit_bytes=24 * 1024 * 1024),
        name="term",
    )(me, parts, *weights)


def swap(block, axis):
    return lax.ppermute(block, axis, [(0, 1), (1, 0)])


def exchange(block, axes):
    return lax.all_to_all(block, axes, split_axis=0, concat_axis=0, tiled=True)


def in_order(blocks, yl, c):
    a, b, d, e = blocks
    a, b = jnp.where(c == 0, a, b), jnp.where(c == 0, b, a)
    d, e = jnp.where(c == 0, d, e), jnp.where(c == 0, e, d)
    low = yl == 0
    return [jnp.where(low, a, d), jnp.where(low, b, e), jnp.where(low, d, a), jnp.where(low, e, b)]


def body(memory, decoder_in, key_weight, value_weight, top_grad):
    zh, x = lax.axis_index("zh"), lax.axis_index("x")
    yl, c = lax.axis_index("yl"), lax.axis_index("c")

    own = jnp.concatenate([key_weight[0], value_weight[0]], axis=1)
    near = swap(own, "c")
    far = swap(own, "yl")

    piece = memory.reshape(2, 2, 2, 2, 128).transpose(0, 1, 3, 2, 4).reshape(1, 16, 128)
    narrow = exchange(jnp.broadcast_to(piece, (32, 16, 128)), ("zh",) + BLOCK)
    narrow = narrow.reshape(4, 128, 128).transpose(1, 0, 2).reshape(1, 128, 512)
    narrow, near, far = lax.optimization_barrier((narrow, near, far))
    weights = [own, near, far, swap(far, "c")]
    every = exchange(jnp.broadcast_to(narrow, (4, 128, 512)), "x")
    rows = every.reshape(4, 128, 4, 128).transpose(1, 2, 0, 3).reshape(128, 2048)
    parts = [jnp.dot(rows, w, preferred_element_type=F32).astype(BF16) for w in weights]
    parts = in_order(parts, yl, c)
    projected = jnp.concatenate([q[:, :64] for q in parts] + [q[:, 64:] for q in parts], axis=1)

    columns = projected.reshape(8, 2, MEM, 512).transpose(1, 0, 2, 3)
    outgoing = jnp.broadcast_to(columns[:, None], (2, 2, 8, MEM, 512)).reshape(32, MEM, 512)
    held = exchange(outgoing, ("zh",) + BLOCK).reshape(1, 4, 8, MEM, 512)
    kv = exchange(jnp.broadcast_to(held, (4, 4, 8, MEM, 512)), "x").reshape(16, 8, MEM, 512)

    mine = (zh // 2, (zh % 2 * 4 + x) * TOKENS, 0)
    h = lax.dynamic_slice(decoder_in, mine, (1, TOKENS, WIDTH))[0]
    g = lax.dynamic_slice(top_grad, mine, (1, TOKENS, WIDTH))[0]
    grads = chain(h, g, kv)

    shares = exchange(grads.reshape(4, 4, 8, MEM, 512), "x")
    summed = jnp.sum(shares.astype(F32), axis=0).astype(BF16)
    parts = exchange(summed.reshape(128, 2, 512), ("zh", "yh", "zl", "yl", "c")).reshape(256, 512)
    pieces = term(jnp.stack([yl, c]), parts, weights).reshape(4, 32, HEADS, 128)
    pieces = jnp.sum(exchange(pieces, "x").astype(F32), axis=0).astype(BF16)
    pieces = exchange(pieces.reshape(32, HEADS, 128), ("zh",) + BLOCK)
    return jnp.sum(pieces.astype(F32), axis=0).reshape(1, WIDTH)


def solution(mesh):
    fine = Mesh(mesh.devices.reshape(4, 4, 4, 2, 2, 2), SECTION + DP)
    placed = (
        P(DP, None, SECTION),
        P(DP, None, None),
        P(SECTION, None, DP),
        P(SECTION, None, DP),
        P(DP, None, None),
    )
    return jax.shard_map(
        body, mesh=fine, in_specs=placed, out_specs=P(SECTION + DP, None), check_vma=False
    )
```

```python
import jax
import jax.numpy as jnp
from jax import lax
from jax.experimental import pallas as pl
from jax.experimental.pallas import tpu as pltpu
from jax.sharding import Mesh
from jax.sharding import PartitionSpec as P

HEADS = 16
HEAD_DIMENSION = 128
SECTIONS = 16
MEM = 8
TOKENS = 8
WIDTH = HEADS * HEAD_DIMENSION
LANES = MEM * HEADS
SECTION = ("zh", "x")
DP = ("yh", "yl", "zl", "c")
BLOCK = ("yh", "zl")
F32 = jnp.float32
BF16 = jnp.bfloat16


def wide_dot(a, b):
    return lax.dot_general(a, b, (((1,), (0,)), ((), ())), preferred_element_type=F32)


def rows_dot(a, b):
    return lax.dot_general(a, b, (((1,), (1,)), ((), ())), preferred_element_type=F32)


def two_parts(x):
    high = x.astype(BF16)
    low = (x - high.astype(F32)).astype(BF16)
    return jnp.concatenate([high, low], axis=0)


def exact_dot(x, b):
    both = wide_dot(two_parts(x), b)
    return both[:TOKENS] + both[TOKENS:]


def others(x):
    return [pltpu.roll(x, k * HEADS, axis=1) for k in range(1, MEM)]


def tree(terms):
    while len(terms) > 1:
        terms = [a + b for a, b in zip(terms[::2], terms[1::2])] + terms[len(terms) // 2 * 2 :]
    return terms[0]


def slot(section):
    return section % 4 * 4 + section // 4


def head_place(head):
    yh, yl, zl = head // 4, head // 2 % 2, head % 2
    return yh * 2 + zl, yl * 128


def chain_kernel(h_ref, g_ref, kv_ref, out_ref, left, right, key_rows, value_rows, hs, gs, sc_s, p_s, ds_s, scale_s, turned):
    root = HEAD_DIMENSION**-0.5
    lane_head = lax.broadcasted_iota(jnp.int32, (HEADS, LANES), 1) % HEADS
    row_head = lax.broadcasted_iota(jnp.int32, (HEADS, LANES), 0)

    def fill(section, turned_offset, straight_offset):
        now = section % 2
        for head in range(HEADS):
            block, lane = head_place(head)
            own = pl.ds(head, MEM, stride=HEADS)
            for offset, target in ((turned_offset, key_rows), (straight_offset, value_rows)):
                start = offset + lane
                target[now, own, :] = kv_ref[slot(section), block, :, start : start + 128].astype(F32)
        columns = key_rows[now].T.astype(BF16).reshape(MEM, HEADS, LANES)
        rows = value_rows[now].astype(BF16).reshape(MEM, HEADS, LANES)
        for head in range(HEADS):
            lanes = slice(head * 128, head * 128 + 128)
            lane_mask = (lane_head == head).astype(F32).astype(BF16)
            row_mask = (row_head == head).astype(F32).astype(BF16)
            left[now, lanes, :] = (columns * lane_mask[None]).reshape(LANES, LANES)
            right[now, :, lanes] = (rows * row_mask[None]).reshape(LANES, LANES)

    fill(0, 0, 256)
    state = h_ref[...]
    for s in range(SECTIONS):
        wide = state.astype(F32)
        hs[s] = wide
        raw = wide_dot(state, left[s % 2])
        scale = lax.rsqrt(jnp.mean(wide * wide, axis=-1, keepdims=True) + 1e-06)
        scores = raw * (scale * root)
        ratios = [jnp.exp(jnp.minimum(o - scores, 80.0)) for o in others(scores)]
        p = 1.0 / (1.0 + tree(ratios))
        sc_s[s] = scores
        p_s[s] = p
        scale_s[s] = jnp.broadcast_to(scale, (TOKENS, LANES))
        if s + 1 < SECTIONS:
            fill(s + 1, 0, 256)
            state = (wide + exact_dot(p, right[s % 2])).astype(BF16)

    fill(SECTIONS - 1, 256, 0)
    grad = g_ref[...]
    for s in reversed(range(SECTIONS)):
        wide = grad.astype(F32)
        gs[s] = wide
        p = p_s[s]
        dp = wide_dot(grad, left[s % 2])
        weighted = p * dp
        ds = p * (dp - tree([weighted] + others(weighted)))
        scale = scale_s[s][:, :1]
        ds_s[s] = ds * (scale_s[s] * root)
        if s > 0:
            fill(s - 1, 256, 0)
            along = jnp.sum(ds * sc_s[s], axis=-1, keepdims=True) * (1.0 / WIDTH)
            du = exact_dot(ds * root, right[s % 2])
            grad = (wide + scale * (du - hs[s] * (scale * along))).astype(BF16)

    row_section = lax.broadcasted_iota(jnp.int32, (LANES, LANES), 0) >> 3
    lane_section = lax.broadcasted_iota(jnp.int32, (LANES, LANES), 1) >> 3
    same = row_section == lane_section
    for coefficients, factors, offset in ((ds_s, hs, 0), (p_s, gs, 256)):
        turned[...] = coefficients[...].reshape(SECTIONS * TOKENS, LANES).T
        for head in range(HEADS):
            mine = turned[pl.ds(head, MEM, stride=HEADS), :]
            spread_out = jnp.broadcast_to(mine[None], (SECTIONS, MEM, LANES)).reshape(LANES, LANES)
            left = jnp.where(same, spread_out, 0.0).astype(BF16)
            lanes = slice(head * 128, head * 128 + 128)
            right = factors[:, :, lanes].reshape(SECTIONS * TOKENS, 128).astype(BF16)
            result = wide_dot(left, right).astype(BF16).reshape(SECTIONS, MEM, 128)
            block, lane = head_place(head)
            start = offset + lane
            for s in range(SECTIONS):
                out_ref[slot(s), block, :, start : start + 128] = result[s]


def chain(h, g, kv):
    vmem = pl.BlockSpec(memory_space=pltpu.VMEM)
    return pl.pallas_call(
        chain_kernel,
        out_shape=jax.ShapeDtypeStruct((SECTIONS, 8, MEM, 512), BF16),
        in_specs=[vmem] * 3,
        out_specs=vmem,
        scratch_shapes=[
            pltpu.VMEM((2, WIDTH, LANES), BF16),
            pltpu.VMEM((2, LANES, WIDTH), BF16),
            pltpu.VMEM((2, LANES, LANES), F32),
            pltpu.VMEM((2, LANES, LANES), F32),
            pltpu.VMEM((SECTIONS, TOKENS, WIDTH), F32),
            pltpu.VMEM((SECTIONS, TOKENS, WIDTH), F32),
            pltpu.VMEM((SECTIONS, TOKENS, LANES), F32),
            pltpu.VMEM((SECTIONS, TOKENS, LANES), F32),
            pltpu.VMEM((SECTIONS, TOKENS, LANES), F32),
            pltpu.VMEM((SECTIONS, TOKENS, LANES), F32),
            pltpu.VMEM((LANES, LANES), F32),
        ],
        compiler_params=pltpu.CompilerParams(vmem_limit_bytes=24 * 1024 * 1024),
        name="sections",
    )(h, g, kv)


def term_kernel(me_ref, part_ref, *refs):
    *weight_refs, out_ref, wide = refs
    yl_set, c_set = me_ref[0] == 1, me_ref[1] == 1
    halves = part_ref[...].astype(F32).reshape(2, 2, 64, 512)
    summed = (halves[:, 0] + halves[:, 1]).reshape(128, 512)
    blocks = [
        jnp.concatenate([summed[:, 64 * q : 64 * q + 64], summed[:, 256 + 64 * q : 320 + 64 * q]], axis=1)
        for q in range(4)
    ]
    a, b, d, e = blocks
    a, b = jnp.where(c_set, b, a), jnp.where(c_set, a, b)
    d, e = jnp.where(c_set, e, d), jnp.where(c_set, d, e)
    a, b, d, e = jnp.where(yl_set, d, a), jnp.where(yl_set, e, b), jnp.where(yl_set, a, d), jnp.where(yl_set, b, e)
    grads = [q.astype(BF16) for q in (a, b, d, e)]
    for start in range(0, WIDTH, 512):
        columns = slice(start, start + 512)
        total = sum(rows_dot(q, ref[columns, :]) for q, ref in zip(grads, weight_refs))
        for lane in range(0, 512, 128):
            wide[pl.ds((start + lane) // 128, 128, stride=HEADS), :] = total[:, lane : lane + 128]
    for row in range(128):
        j, yh, zl, yl, c, m = (row >> k & n for k, n in ((6, 1), (4, 3), (3, 1), (2, 1), (1, 1), (0, 1)))
        owner = ((yl * 2 + zl) * 4 + yh) * 8 + (c * 2 + j) * 2 + m
        out_ref[owner] = wide[row * HEADS : (row + 1) * HEADS, :].astype(BF16)


def term(me, parts, weights):
    vmem = pl.BlockSpec(memory_space=pltpu.VMEM)
    return pl.pallas_call(
        term_kernel,
        out_shape=jax.ShapeDtypeStruct((128, HEADS, 128), BF16),
        in_specs=[pl.BlockSpec(memory_space=pltpu.SMEM)] + [vmem] * (1 + len(weights)),
        out_specs=vmem,
        scratch_shapes=[pltpu.VMEM((128 * HEADS, 128), F32)],
        compiler_params=pltpu.CompilerParams(vmem_limit_bytes=24 * 1024 * 1024),
        name="term",
    )(me, parts, *weights)


def swap(block, axis):
    return lax.ppermute(block, axis, [(0, 1), (1, 0)])


def exchange(block, axes):
    return lax.all_to_all(block, axes, split_axis=0, concat_axis=0, tiled=True)


def in_order(blocks, yl, c):
    a, b, d, e = blocks
    a, b = jnp.where(c == 0, a, b), jnp.where(c == 0, b, a)
    d, e = jnp.where(c == 0, d, e), jnp.where(c == 0, e, d)
    low = yl == 0
    return [jnp.where(low, a, d), jnp.where(low, b, e), jnp.where(low, d, a), jnp.where(low, e, b)]


def body(memory, decoder_in, key_weight, value_weight, top_grad):
    zh, x = lax.axis_index("zh"), lax.axis_index("x")
    yl, c = lax.axis_index("yl"), lax.axis_index("c")

    own = jnp.concatenate([key_weight[0], value_weight[0]], axis=1)
    near = swap(own, "c")
    far = swap(own, "yl")

    mine = (zh // 2, (zh % 2 * 4 + x) * TOKENS, 0)
    h = lax.dynamic_slice(decoder_in, mine, (1, TOKENS, WIDTH))[0]
    g = lax.dynamic_slice(top_grad, mine, (1, TOKENS, WIDTH))[0]

    piece = memory.reshape(2, 2, 2, 2, 128).transpose(0, 1, 3, 2, 4).reshape(1, 16, 128)
    narrow = exchange(jnp.broadcast_to(piece, (32, 16, 128)), ("zh",) + BLOCK)
    narrow = narrow.reshape(4, 128, 128).transpose(1, 0, 2).reshape(1, 128, 512)
    narrow, near, far = lax.optimization_barrier((narrow, near, far))
    weights = [own, near, far, swap(far, "c")]
    every = exchange(jnp.broadcast_to(narrow, (4, 128, 512)), "x")
    every, h, g, me = lax.optimization_barrier((every, h, g, jnp.stack([yl, c])))
    rows = every.reshape(4, 128, 4, 128).transpose(1, 2, 0, 3).reshape(128, 2048)
    parts = [jnp.dot(rows, w, preferred_element_type=F32).astype(BF16) for w in weights]
    parts = in_order(parts, yl, c)
    projected = jnp.concatenate([q[:, :64] for q in parts] + [q[:, 64:] for q in parts], axis=1)

    columns = projected.reshape(8, 2, MEM, 512).transpose(1, 0, 2, 3)
    outgoing = jnp.broadcast_to(columns[:, None], (2, 2, 8, MEM, 512)).reshape(32, MEM, 512)
    held = exchange(outgoing, ("zh",) + BLOCK).reshape(1, 4, 8, MEM, 512)
    kv = exchange(jnp.broadcast_to(held, (4, 4, 8, MEM, 512)), "x").reshape(16, 8, MEM, 512)

    grads = chain(h, g, kv)

    shares = exchange(grads.reshape(4, 4, 8, MEM, 512), "x")
    summed = jnp.sum(shares.astype(F32), axis=0).astype(BF16)
    parts = exchange(summed.reshape(128, 2, 512), ("zh", "yh", "zl", "yl", "c")).reshape(256, 512)
    pieces = term(me, parts, weights).reshape(4, 32, HEADS, 128)
    pieces = jnp.sum(exchange(pieces, "x").astype(F32), axis=0).astype(BF16)
    pieces = exchange(pieces.reshape(32, HEADS, 128), ("zh",) + BLOCK)
    return jnp.sum(pieces.astype(F32), axis=0).reshape(1, WIDTH)


def solution(mesh):
    fine = Mesh(mesh.devices.reshape(4, 4, 4, 2, 2, 2), SECTION + DP)
    placed = (
        P(DP, None, SECTION),
        P(DP, None, None),
        P(SECTION, None, DP),
        P(SECTION, None, DP),
        P(DP, None, None),
    )
    return jax.shard_map(
        body, mesh=fine, in_specs=placed, out_specs=P(SECTION + DP, None), check_vma=False
    )
```

```python
import jax
import jax.numpy as jnp
from jax import lax
from jax.experimental import pallas as pl
from jax.experimental.pallas import tpu as pltpu
from jax.sharding import Mesh
from jax.sharding import PartitionSpec as P

HEADS = 16
HEAD_DIMENSION = 128
SECTIONS = 16
MEM = 8
TOKENS = 8
WIDTH = HEADS * HEAD_DIMENSION
LANES = MEM * HEADS
SECTION = ("zh", "x")
DP = ("yh", "yl", "zl", "c")
BLOCK = ("yh", "zl")
F32 = jnp.float32
BF16 = jnp.bfloat16


def wide_dot(a, b):
    return lax.dot_general(a, b, (((1,), (0,)), ((), ())), preferred_element_type=F32)


def rows_dot(a, b):
    return lax.dot_general(a, b, (((1,), (1,)), ((), ())), preferred_element_type=F32)


def two_parts(x):
    high = x.astype(BF16)
    low = (x - high.astype(F32)).astype(BF16)
    return jnp.concatenate([high, low], axis=0)


def exact_dot(x, b):
    both = wide_dot(two_parts(x), b)
    return both[:TOKENS] + both[TOKENS:]


def others(x):
    return [pltpu.roll(x, k * HEADS, axis=1) for k in range(1, MEM)]


def tree(terms):
    while len(terms) > 1:
        terms = [a + b for a, b in zip(terms[::2], terms[1::2])] + terms[len(terms) // 2 * 2 :]
    return terms[0]


def slot(section):
    return section % 4 * 4 + section // 4


def head_place(head):
    yh, yl, zl = head // 4, head // 2 % 2, head % 2
    return yh * 2 + zl, yl * 128


def chain_kernel(h_ref, g_ref, kv_ref, out_ref, left, right, key_rows, value_rows, hs, gs, sc_s, p_s, ds_s, scale_s, turned):
    root = HEAD_DIMENSION**-0.5
    lane_head = lax.broadcasted_iota(jnp.int32, (HEADS, LANES), 1) % HEADS
    row_head = lax.broadcasted_iota(jnp.int32, (HEADS, LANES), 0)

    def fill(section, turned_offset, straight_offset):
        now = section % 2
        for head in range(HEADS):
            block, lane = head_place(head)
            own = pl.ds(head, MEM, stride=HEADS)
            for offset, target in ((turned_offset, key_rows), (straight_offset, value_rows)):
                start = offset + lane
                target[now, own, :] = kv_ref[slot(section), block, :, start : start + 128].astype(F32)
        columns = key_rows[now].T.astype(BF16).reshape(MEM, HEADS, LANES)
        rows = value_rows[now].astype(BF16).reshape(MEM, HEADS, LANES)
        for head in range(HEADS):
            lanes = slice(head * 128, head * 128 + 128)
            lane_mask = (lane_head == head).astype(F32).astype(BF16)
            row_mask = (row_head == head).astype(F32).astype(BF16)
            left[now, lanes, :] = (columns * lane_mask[None]).reshape(LANES, LANES)
            right[now, :, lanes] = (rows * row_mask[None]).reshape(LANES, LANES)

    fill(0, 0, 256)
    state = h_ref[...]
    for s in range(SECTIONS):
        wide = state.astype(F32)
        hs[s] = wide
        raw = wide_dot(state, left[s % 2])
        scale = lax.rsqrt(jnp.mean(wide * wide, axis=-1, keepdims=True) + 1e-06)
        scores = raw * (scale * root)
        ratios = [jnp.exp(jnp.minimum(o - scores, 80.0)) for o in others(scores)]
        p = 1.0 / (1.0 + tree(ratios))
        sc_s[s] = scores
        p_s[s] = p
        scale_s[s] = jnp.broadcast_to(scale, (TOKENS, LANES))
        if s + 1 < SECTIONS:
            fill(s + 1, 0, 256)
            state = (wide + exact_dot(p, right[s % 2])).astype(BF16)

    fill(SECTIONS - 1, 256, 0)
    grad = g_ref[...]
    for s in reversed(range(SECTIONS)):
        wide = grad.astype(F32)
        gs[s] = wide
        p = p_s[s]
        dp = wide_dot(grad, left[s % 2])
        weighted = p * dp
        ds = p * (dp - tree([weighted] + others(weighted)))
        scale = scale_s[s][:, :1]
        ds_s[s] = ds * (scale_s[s] * root)
        if s > 0:
            fill(s - 1, 256, 0)
            along = jnp.sum(ds * sc_s[s], axis=-1, keepdims=True) * (1.0 / WIDTH)
            du = exact_dot(ds * root, right[s % 2])
            grad = (wide + scale * (du - hs[s] * (scale * along))).astype(BF16)

    row_section = lax.broadcasted_iota(jnp.int32, (LANES, LANES), 0) >> 3
    lane_section = lax.broadcasted_iota(jnp.int32, (LANES, LANES), 1) >> 3
    same = row_section == lane_section
    for coefficients, factors, offset in ((ds_s, hs, 0), (p_s, gs, 256)):
        turned[...] = coefficients[...].reshape(SECTIONS * TOKENS, LANES).T
        for head in range(HEADS):
            mine = turned[pl.ds(head, MEM, stride=HEADS), :]
            spread_out = jnp.broadcast_to(mine[None], (SECTIONS, MEM, LANES)).reshape(LANES, LANES)
            left = jnp.where(same, spread_out, 0.0).astype(BF16)
            lanes = slice(head * 128, head * 128 + 128)
            right = factors[:, :, lanes].reshape(SECTIONS * TOKENS, 128).astype(BF16)
            result = wide_dot(left, right).astype(BF16).reshape(SECTIONS, MEM, 128)
            block, lane = head_place(head)
            start = offset + lane
            for s in range(SECTIONS):
                out_ref[slot(s), block, :, start : start + 128] = result[s]


def chain(h, g, kv):
    vmem = pl.BlockSpec(memory_space=pltpu.VMEM)
    return pl.pallas_call(
        chain_kernel,
        out_shape=jax.ShapeDtypeStruct((SECTIONS, 8, MEM, 512), BF16),
        in_specs=[vmem] * 3,
        out_specs=vmem,
        scratch_shapes=[
            pltpu.VMEM((2, WIDTH, LANES), BF16),
            pltpu.VMEM((2, LANES, WIDTH), BF16),
            pltpu.VMEM((2, LANES, LANES), F32),
            pltpu.VMEM((2, LANES, LANES), F32),
            pltpu.VMEM((SECTIONS, TOKENS, WIDTH), F32),
            pltpu.VMEM((SECTIONS, TOKENS, WIDTH), F32),
            pltpu.VMEM((SECTIONS, TOKENS, LANES), F32),
            pltpu.VMEM((SECTIONS, TOKENS, LANES), F32),
            pltpu.VMEM((SECTIONS, TOKENS, LANES), F32),
            pltpu.VMEM((SECTIONS, TOKENS, LANES), F32),
            pltpu.VMEM((LANES, LANES), F32),
        ],
        compiler_params=pltpu.CompilerParams(vmem_limit_bytes=24 * 1024 * 1024),
        name="sections",
    )(h, g, kv)


def term_kernel(me_ref, part_ref, *refs):
    *weight_refs, out_ref, wide = refs
    yl_set, c_set = me_ref[0] == 1, me_ref[1] == 1
    halves = part_ref[...].astype(F32).reshape(2, 2, 64, 512)
    summed = (halves[:, 0] + halves[:, 1]).reshape(128, 512)
    blocks = [
        jnp.concatenate([summed[:, 64 * q : 64 * q + 64], summed[:, 256 + 64 * q : 320 + 64 * q]], axis=1)
        for q in range(4)
    ]
    a, b, d, e = blocks
    a, b = jnp.where(c_set, b, a), jnp.where(c_set, a, b)
    d, e = jnp.where(c_set, e, d), jnp.where(c_set, d, e)
    a, b, d, e = jnp.where(yl_set, d, a), jnp.where(yl_set, e, b), jnp.where(yl_set, a, d), jnp.where(yl_set, b, e)
    grads = [q.astype(BF16) for q in (a, b, d, e)]
    for start in range(0, WIDTH, 512):
        columns = slice(start, start + 512)
        total = sum(rows_dot(q, ref[columns, :]) for q, ref in zip(grads, weight_refs))
        for lane in range(0, 512, 128):
            wide[pl.ds((start + lane) // 128, 128, stride=HEADS), :] = total[:, lane : lane + 128]
    for row in range(128):
        j, yh, zl, yl, c, m = (row >> k & n for k, n in ((6, 1), (4, 3), (3, 1), (2, 1), (1, 1), (0, 1)))
        owner = ((yl * 2 + zl) * 4 + yh) * 8 + (c * 2 + j) * 2 + m
        out_ref[owner] = wide[row * HEADS : (row + 1) * HEADS, :].astype(BF16)


def term(me, parts, weights):
    vmem = pl.BlockSpec(memory_space=pltpu.VMEM)
    return pl.pallas_call(
        term_kernel,
        out_shape=jax.ShapeDtypeStruct((128, HEADS, 128), BF16),
        in_specs=[pl.BlockSpec(memory_space=pltpu.SMEM)] + [vmem] * (1 + len(weights)),
        out_specs=vmem,
        scratch_shapes=[pltpu.VMEM((128 * HEADS, 128), F32)],
        compiler_params=pltpu.CompilerParams(vmem_limit_bytes=24 * 1024 * 1024),
        name="term",
    )(me, parts, *weights)


def swap(block, axis):
    return lax.ppermute(block, axis, [(0, 1), (1, 0)])


def exchange(block, axes):
    return lax.all_to_all(block, axes, split_axis=0, concat_axis=0, tiled=True)


def in_order(blocks, yl, c):
    a, b, d, e = blocks
    a, b = jnp.where(c == 0, a, b), jnp.where(c == 0, b, a)
    d, e = jnp.where(c == 0, d, e), jnp.where(c == 0, e, d)
    low = yl == 0
    return [jnp.where(low, a, d), jnp.where(low, b, e), jnp.where(low, d, a), jnp.where(low, e, b)]


def body(memory, decoder_in, key_weight, value_weight, top_grad):
    zh, x = lax.axis_index("zh"), lax.axis_index("x")
    yl, c = lax.axis_index("yl"), lax.axis_index("c")

    own = jnp.concatenate([key_weight[0], value_weight[0]], axis=1)
    near = swap(own, "c")
    far = swap(own, "yl")

    mine = (zh // 2, (zh % 2 * 4 + x) * TOKENS, 0)
    h = lax.dynamic_slice(decoder_in, mine, (1, TOKENS, WIDTH))[0]
    g = lax.dynamic_slice(top_grad, mine, (1, TOKENS, WIDTH))[0]

    piece = memory.reshape(2, 2, 2, 2, 128).transpose(0, 1, 3, 2, 4).reshape(1, 16, 128)
    narrow = exchange(jnp.broadcast_to(piece, (32, 16, 128)), ("zh",) + BLOCK)
    narrow = narrow.reshape(4, 128, 128).transpose(1, 0, 2).reshape(1, 128, 512)
    weights = [own, near, far, swap(far, "c")]
    every = exchange(jnp.broadcast_to(narrow, (4, 128, 512)), "x")
    every, h, g, me = lax.optimization_barrier((every, h, g, jnp.stack([yl, c])))
    rows = every.reshape(4, 128, 4, 128).transpose(1, 2, 0, 3).reshape(128, 2048)
    parts = [jnp.dot(rows, w, preferred_element_type=F32).astype(BF16) for w in weights]
    parts = in_order(parts, yl, c)
    projected = jnp.concatenate([q[:, :64] for q in parts] + [q[:, 64:] for q in parts], axis=1)

    columns = projected.reshape(8, 2, MEM, 512).transpose(1, 0, 2, 3)
    outgoing = jnp.broadcast_to(columns[:, None], (2, 2, 8, MEM, 512)).reshape(32, MEM, 512)
    held = exchange(outgoing, ("zh",) + BLOCK).reshape(1, 4, 8, MEM, 512)
    kv = exchange(jnp.broadcast_to(held, (4, 4, 8, MEM, 512)), "x").reshape(16, 8, MEM, 512)

    grads = chain(h, g, kv)

    shares = exchange(grads.reshape(4, 4, 8, MEM, 512), "x")
    summed = jnp.sum(shares.astype(F32), axis=0).astype(BF16)
    parts = exchange(summed.reshape(128, 2, 512), ("zh", "yh", "zl", "yl", "c")).reshape(256, 512)
    pieces = term(me, parts, weights).reshape(4, 32, HEADS, 128)
    pieces = jnp.sum(exchange(pieces, "x").astype(F32), axis=0).astype(BF16)
    pieces = exchange(pieces.reshape(32, HEADS, 128), ("zh",) + BLOCK)
    return jnp.sum(pieces.astype(F32), axis=0).reshape(1, WIDTH)


def solution(mesh):
    fine = Mesh(mesh.devices.reshape(4, 4, 4, 2, 2, 2), SECTION + DP)
    placed = (
        P(DP, None, SECTION),
        P(DP, None, None),
        P(SECTION, None, DP),
        P(SECTION, None, DP),
        P(DP, None, None),
    )
    return jax.shard_map(
        body, mesh=fine, in_specs=placed, out_specs=P(SECTION + DP, None), check_vma=False
    )
```
